512 devices in a mesh: section: 16 (over x_hi, z), kvp: 16 (over x_lo, y), tp: 2 (over core).
Axes of the slice: x: 4 (x_hi: 2, x_lo: 2; x = x_hi * 2 + x_lo), y: 8, z: 8, core: 2. Of those that a mesh axis runs over, the one named last changes fastest.
Arguments:
- entering: bfloat16 [16, 128, 4096], P('section', 'tp', 'kvp'), may hold values from -6 to 6
- feed: bfloat16 [1, 128, 4096], P(None, 'tp', 'kvp'), may hold values from -6 to 6
- gain: float32 [16, 4096], P('section'), may hold values from 0.5 to 1.5
- wq: bfloat16 [16, 4096, 2, 2048], P('section', None, 'tp', 'kvp'), may hold values from -0.09375 to 0.09375
- wkv: bfloat16 [16, 4096, 2, 512], P('section', None, 'tp', 'kvp'), may hold values from -0.21875 to 0.21875
- wo: bfloat16 [16, 4096, 4096], P('section', 'tp', 'kvp'), may hold values from -0.09375 to 0.09375
- cache: bfloat16 [16, 2, 4, 8192, 128], P('section', None, 'tp', 'kvp'), may hold values from -180 to 180
- prefix_len: int32 [16, 16], P('section', 'kvp'), may hold values from 1 to 256, as said below
- owner: int32 [2, 16], P(None, 'section'), may hold values from 0 to 15
Outputs:
- states: bfloat16 [2, 16, 128, 4096], P(None, 'section', 'tp', 'kvp')
- new_cache: bfloat16 [16, 2, 4, 8192, 128], P('section', None, 'tp', 'kvp')
The draws below stay inside these ranges and needn't reach their ends.
Inputs may be any that keep to these rules, and one draw needn't show every extreme that they name: `prefix_len`: in every layer some shard holds exactly 256 filled slots.
All inputs are finite; a program needn't handle non-finite values.
Results may differ from the reference program's by a relative error of at most 0.03.
The reference program's roundings to bfloat16 on the way count: a program that leaves them out, or rounds other values in their place, can miss the bound.
Values may be sent and summed in bfloat16 or wider, within the bound.
No kernel may reach another device: no remote copies, remote signals or barrier semaphores. Data moves between devices by JAX's collectives and lax.ppermute only.
A program may use at most 128 MiB of HBM per device.

```python
import math
import jax
import jax.numpy as jnp
from jax import lax

D = 4096
H = 32
KVH = 4
HD = 128
NCH = 2
SPAN = 128
CAP = 512
LAYERS = 16
SHARDS = 16
KV_SLOTS = 8192
N_KVP = 16


def draw_cache(key, part):
    key = jax.random.fold_in(key, 7)
    shape = (LAYERS, 2, KVH, KV_SLOTS, HD)
    first_key = jax.random.fold_in(key, 0)
    kind_scale = jnp.array([2.5, 1.0], jnp.float32).reshape(1, 2, 1, 1, 1)
    base = jax.random.truncated_normal(first_key, -6.0, 6.0, shape, jnp.float32)
    return (base * kind_scale).astype(jnp.bfloat16)


def draw_prefix_len(key, part):
    key = jax.random.fold_in(key, 5)
    first_key, second_key = jax.random.split(key)
    largest = CAP - NCH * SPAN
    values = jax.random.randint(first_key, (LAYERS, SHARDS), 1, largest + 1)
    chosen = jax.random.randint(second_key, (LAYERS, 1), 0, SHARDS)
    columns = jnp.arange(SHARDS, dtype=jnp.int32)[None, :]
    return jnp.where(columns == chosen, largest, values).astype(jnp.int32)


def touch_ends(values, stream_key, least, high):
    shape = values.shape
    index_at = [jax.random.randint(jax.random.fold_in(stream_key, axis), (), 0, shape[axis]) for axis in range(len(shape))]
    values = values.at[tuple(index_at)].set(least)
    longest = shape.index(max(shape))
    index_at[longest] = (index_at[longest] + 1) % shape[longest]
    return values.at[tuple(index_at)].set(high)


def steps_of(rng, extent, cuts, low, top_value):
    factor_of, own = 1.0, jax.random.fold_in(rng, 6)
    for dim, blocks in cuts:
        heights = jnp.exp(jax.random.uniform(jax.random.fold_in(own, dim), (blocks,), jnp.float32, low / len(cuts), top_value / len(cuts)))
        factor_of = factor_of * jnp.repeat(heights, extent[dim] // blocks).reshape([-1 if axis == dim else 1 for axis in range(len(extent))])
    return factor_of


def noise(own_key, shape, spread, limit, pieces=(), kind=jnp.bfloat16):
    factor_of = steps_of(own_key, shape, pieces, -0.22, 0.18) if pieces else 1.0
    values = jax.random.normal(own_key, shape, jnp.float32) * spread * factor_of
    return jnp.minimum(jnp.maximum(values, -limit), limit).astype(kind)


def setup_inputs(seed: int = 0) -> dict:
    streams_of = jax.random.split(jax.random.key(seed), 10)
    return {
        "entering": noise(streams_of[0], (LAYERS, SPAN, D), 1.0, 6.0, ((0, 16), (1, 2), (2, 16))),
        "feed": noise(streams_of[1], (NCH - 1, SPAN, D), 1.0, 6.0, ((1, 2), (2, 16))),
        "gain": jnp.clip(1.0 + 0.1 * jax.random.normal(streams_of[2], (LAYERS, D), jnp.float32), 0.5, 1.5),
        "wq": noise(streams_of[3], (LAYERS, D, 2, H * HD // 2), D ** -0.5, 0.09375, ((0, 16), (2, 2), (3, 16))),
        "wkv": noise(streams_of[4], (LAYERS, D, 2, KVH * HD), (D // 6) ** -0.5, 0.21875, ((0, 16), (2, 2), (3, 16))),
        "wo": noise(streams_of[5], (LAYERS, H * HD, D), (H * HD) ** -0.5, 0.09375, ((0, 16), (1, 2), (2, 16))),
        "cache": draw_cache(jax.random.fold_in(streams_of[9], 71), 0),
        "prefix_len": draw_prefix_len(jax.random.fold_in(streams_of[9], 71), 0),
        "owner": touch_ends(jax.random.randint(streams_of[8], (NCH, LAYERS), 0, SHARDS), jax.random.fold_in(streams_of[8], 1), 0, SHARDS - 1).astype(jnp.int32),
    }


EPS = 1e-05

def one_layer(inputs, gain_row, wq_layer, wkv_layer, wo_layer, cache_layer, filled, owner_now):
    widened = inputs.astype(jnp.float32)
    normed = (widened * lax.rsqrt(lax.optimization_barrier(jnp.mean(widened * widened, axis=-1, keepdims=True)) + EPS) * gain_row).astype(jnp.bfloat16)
    queries = jnp.dot(normed, wq_layer.reshape(D, H * HD), preferred_element_type=jnp.float32).astype(jnp.bfloat16)
    keyvals = jnp.dot(normed, wkv_layer.reshape(D, 2 * KVH * HD), preferred_element_type=jnp.float32).astype(jnp.bfloat16)
    keyvals = keyvals.reshape(SPAN, KVH, 2, HD)
    fresh = jnp.transpose(keyvals, (2, 1, 0, 3))
    anchor = jnp.zeros((), jnp.int32)
    start = (owner_now * CAP + filled[owner_now]).astype(jnp.int32)
    cache_layer = lax.dynamic_update_slice(cache_layer, fresh, (anchor, anchor, start, anchor))
    group_size = H // KVH
    score_scale = 1.0 / math.sqrt(HD)
    query_heads = queries.reshape(SPAN, KVH, group_size, HD).astype(jnp.float32)
    row_index = jnp.arange(SPAN, dtype=jnp.int32)
    slot_index = jnp.arange(CAP, dtype=jnp.int32)

    def shard_part(shard_id):
        block = lax.dynamic_slice_in_dim(cache_layer, (shard_id * CAP).astype(jnp.int32), CAP, 2)
        keys = block[0].astype(jnp.float32)
        values = block[1].astype(jnp.float32)
        scores = jnp.einsum('rkgd,kpd->rkgp', query_heads, keys) * score_scale
        limits = filled[shard_id] + jnp.where(shard_id == owner_now, row_index + 1, 0)
        visible = (slot_index[None, :] < limits[:, None])[:, None, None, :]
        masked = jnp.where(visible, scores, -1e+30)
        maxima = lax.optimization_barrier(jnp.max(masked, axis=-1))
        expon = jnp.where(visible, jnp.exp(masked - maxima[..., None]), 0.0)
        denoms = lax.optimization_barrier(jnp.sum(expon, axis=-1))
        probs = lax.optimization_barrier(expon.astype(jnp.bfloat16)).astype(jnp.float32)
        partial_out = jnp.einsum('rkgp,kpd->rkgd', probs, values)
        return (maxima, denoms, partial_out)
    maxima, denoms, partial_out = lax.map(shard_part, jnp.arange(N_KVP, dtype=jnp.int32))
    top_max = lax.optimization_barrier(jnp.max(maxima, axis=0))
    weights = jnp.exp(maxima - top_max)
    totals = lax.optimization_barrier(jnp.sum(weights * denoms, axis=0))
    attended = lax.optimization_barrier(jnp.sum(weights[..., None] * partial_out, axis=0)) / totals[..., None]
    attended = attended.reshape(SPAN, H * HD).astype(jnp.bfloat16)
    mixed_out = jnp.dot(attended, wo_layer, preferred_element_type=jnp.float32)
    return ((widened + mixed_out).astype(jnp.bfloat16), cache_layer)

def reference(entering, feed, gain, wq, wkv, wo, cache, prefix_len, owner):
    caches = [cache[layer_id] for layer_id in range(LAYERS)]
    fills = [prefix_len[layer_id] for layer_id in range(LAYERS)]
    shard_ids = jnp.arange(N_KVP, dtype=jnp.int32)
    outputs = []
    previous = None
    for moment in range(NCH):
        current = []
        for layer_id in range(LAYERS):
            if moment == 0:
                inputs = entering[layer_id]
            elif layer_id == 0:
                inputs = feed[moment - 1]
            else:
                inputs = previous[layer_id - 1]
            owner_now = owner[moment, layer_id]
            result, caches[layer_id] = one_layer(inputs, gain[layer_id], wq[layer_id], wkv[layer_id], wo[layer_id], caches[layer_id], fills[layer_id], owner_now)
            fills[layer_id] = fills[layer_id] + jnp.where(shard_ids == owner_now, SPAN, 0).astype(jnp.int32)
            current.append(result)
        outputs.append(jnp.stack(current))
        previous = current
    return (jnp.stack(outputs), jnp.stack(caches))
```

```python
import functools
import math

import jax
import jax.numpy as jnp
from jax import lax
from jax.experimental import pallas as pl
from jax.experimental.pallas import tpu as pltpu
from jax.sharding import PartitionSpec as P

HD = 128
NCH = 2
EPS = 1e-05
N = 16
RING = 8
ROWS = 64
SPAN = 128
PRE = 256
D = 4096
COLS = 256
SCALE = 1.0 / math.sqrt(HD)
LOW = -1e30
F32 = jnp.float32
BF16 = jnp.bfloat16
RINGS = [list(range(RING)), list(range(RING, N))]
VMEM = pl.BlockSpec(memory_space=pltpu.VMEM)
SMEM = pl.BlockSpec(memory_space=pltpu.SMEM)
PARAMS = pltpu.CompilerParams(vmem_limit_bytes=40 * 1024 * 1024)


def dot(a, b):
    return jnp.dot(a, b, preferred_element_type=F32)


def dot_t(a, b):
    return lax.dot_general(a, b, (((1,), (1,)), ((), ())), preferred_element_type=F32)


def normalise(place, mine, other, gain, normed):
    t = place[0]
    for half, ref in ((t, mine), (1 - t, other)):
        total = jnp.zeros((ROWS, COLS), F32)
        for j in range(N):
            part = ref[j].astype(F32)
            total = total + part * part
        inverse = lax.rsqrt(jnp.sum(total, axis=1, keepdims=True) / D + EPS)
        rows = pl.ds(pl.multiple_of(half * ROWS, ROWS), ROWS)
        for j in range(N):
            cols = slice(j * COLS, (j + 1) * COLS)
            normed[rows, cols] = (ref[j].astype(F32) * inverse * gain[:, cols]).astype(BF16)


def project_first(place, lens, mine, other, gain, wq, wkv, q_out, kv_out, normed):
    normalise(place, mine, other, gain, normed)
    q_out[...] = dot(normed[...], wq[...]).astype(BF16)
    kv = dot(normed[...], wkv[...]).T.astype(BF16)
    filled = jnp.full((16, SPAN), lens[0].astype(F32), F32).astype(BF16)
    for j in range(N):
        kv_out[j, 0:32] = kv
        kv_out[j, 32:48] = filled


def project_later(place, mine, other, gain, wq, wkv, q_out, kv_out, normed):
    normalise(place, mine, other, gain, normed)
    q_out[...] = dot(normed[...], wq[...]).astype(BF16)
    kv_out[...] = dot_t(normed[...], wkv[...]).astype(BF16)


def attend(place, q_ref, held, first, *rest, later):
    if later:
        second, out, scores = rest
    else:
        out, scores = rest
    g = place[1]
    q = q_ref[...]
    slot = lax.broadcasted_iota(jnp.int32, (1, PRE), 1).astype(F32)
    top = jnp.full((SPAN, PRE), LOW, F32)
    for k in range(RING):
        for o in range(2):
            shard = (g if o == 0 else 1 - g) * RING + k
            filled = first[shard, 32:48][0:1].astype(F32)
            filled = jnp.concatenate([filled, filled], axis=1)
            s = dot_t(q, held[k, o, 0]) * SCALE
            s = jnp.where(slot < filled, s, LOW)
            b = (k * 2 + o) * PRE
            scores[:, b : b + PRE] = s
            top = jnp.maximum(top, s)
    top = jnp.max(top, axis=1, keepdims=True)
    row = lax.broadcasted_iota(jnp.int32, (SPAN, SPAN), 0)
    col = lax.broadcasted_iota(jnp.int32, (SPAN, SPAN), 1)
    keys = jnp.concatenate([first[g * RING + i, 0:32] for i in range(4)], axis=0)
    values = jnp.concatenate([first[g * RING + 4 + i, 0:32] for i in range(4)], axis=0)
    fresh = [dot(q, keys) * SCALE]
    if later:
        fresh.append(dot_t(q, second[:, 0:HD]) * SCALE)
    fresh[-1] = jnp.where(col <= row, fresh[-1], LOW)
    for s in fresh:
        top = jnp.maximum(top, jnp.max(s, axis=1, keepdims=True))
    total = jnp.zeros((SPAN, PRE), F32)
    acc = jnp.zeros((SPAN, HD), F32)
    for k in range(RING):
        for o in range(2):
            b = (k * 2 + o) * PRE
            e = jnp.exp(scores[:, b : b + PRE] - top)
            total = total + e
            acc = acc + dot(e.astype(BF16), held[k, o, 1])
    total = jnp.sum(total, axis=1, keepdims=True)
    for i, s in enumerate(fresh):
        e = jnp.exp(s - top)
        total = total + jnp.sum(e, axis=1, keepdims=True)
        if i == 0:
            acc = acc + dot_t(e.astype(BF16), values)
        else:
            acc = acc + dot(e.astype(BF16), second[:, HD : 2 * HD])
    result = (acc / total).astype(BF16)
    for j in range(N):
        out[j] = result


def mix(place, att, wo, x_ref, mine, other):
    t = place[0]
    acc = jnp.zeros((SPAN, COLS), F32)
    for j in range(N):
        acc = acc + dot(att[j], wo[j * HD : (j + 1) * HD, :])
    top, bottom = acc[0:ROWS], acc[ROWS:SPAN]
    mine[...] = x_ref[...].astype(F32) + jnp.where(t == 0, top, bottom)
    other[...] = jnp.where(t == 0, bottom, top)


def spread(block):
    return lax.all_to_all(block, "kvp", 0, 0, tiled=True)


def swap(block):
    return lax.ppermute(block, "tp", [(0, 1), (1, 0)])


def shape(*dims, dtype=BF16):
    return jax.ShapeDtypeStruct(dims, dtype)


def body(entering, feed, gain, wq, wkv, wo, cache, prefix_len, owner):
    shard_id = lax.axis_index("kvp")
    section_id = lax.axis_index("section")
    g = shard_id // RING
    place = jnp.stack([lax.axis_index("tp"), g]).astype(jnp.int32)
    filled = prefix_len[0, 0]
    wq_here, wkv_here, wo_here = wq[0, :, 0, :], wkv[0, :, 0, :], wo[0]
    cache_here = cache[0]

    prefix = cache_here[:, :, :PRE, :]
    own = lax.dynamic_index_in_dim(prefix, g, 1, False)
    give = lax.dynamic_index_in_dim(prefix, 1 - g, 1, False)
    got = lax.ppermute(give, "kvp", [(i, (i + RING) % N) for i in range(N)])
    held = lax.all_gather(jnp.stack([own, got]), "kvp", axis_index_groups=RINGS)

    wkv_t, held = lax.optimization_barrier((wkv_here.T, held))
    wkv_all = lax.all_gather(wkv_t, "kvp", axis_index_groups=RINGS).reshape(2 * HD, D)

    outputs, fresh_all = [], []
    x = entering[0]
    for moment in range(NCH):
        if moment:
            passed = lax.ppermute(outputs[-1], "section", [(i, i + 1) for i in range(15)])
            x = jnp.where(section_id == 0, feed[moment - 1], passed)
        mine = spread(jnp.broadcast_to(x[None], (N, ROWS, COLS)))
        other = swap(mine)
        scratch = [pltpu.VMEM((SPAN, D), BF16)]
        if moment == 0:
            q, kv = pl.pallas_call(
                project_first,
                out_shape=(shape(SPAN, HD), shape(N, 48, SPAN)),
                in_specs=[SMEM, SMEM] + [VMEM] * 5,
                out_specs=(VMEM, VMEM),
                scratch_shapes=scratch,
                compiler_params=PARAMS,
                name="project_first",
            )(place, filled[None], mine, other, gain, wq_here, wkv_here)
            first = spread(kv)
            extra = (first,)
            both = jnp.transpose(first[:, 0:32].reshape(2, 2, HD, SPAN), (1, 0, 3, 2))
        else:
            q, kv = pl.pallas_call(
                project_later,
                out_shape=(shape(SPAN, HD), shape(SPAN, 2 * HD)),
                in_specs=[SMEM] + [VMEM] * 5,
                out_specs=(VMEM, VMEM),
                scratch_shapes=scratch,
                compiler_params=PARAMS,
                name="project_later",
            )(place, mine, other, gain, wq_here, wkv_all)
            extra = (first, kv)
            pair = lax.ppermute(kv, "kvp", [(i, (i + RING) % N) for i in range(N)])
            heads = jnp.where(g == 0, jnp.stack([kv, pair]), jnp.stack([pair, kv]))
            both = jnp.transpose(heads.reshape(2, SPAN, 2, HD), (2, 0, 1, 3))
        fresh_all.append(both)
        att = pl.pallas_call(
            functools.partial(attend, later=moment > 0),
            out_shape=shape(N, SPAN, HD),
            in_specs=[SMEM] + [VMEM] * (2 + len(extra)),
            out_specs=VMEM,
            scratch_shapes=[pltpu.VMEM((SPAN, N * PRE), F32)],
            compiler_params=PARAMS,
            name="attend",
        )(place, q, held, *extra)
        att = spread(att)
        own_sum, other_sum = pl.pallas_call(
            mix,
            out_shape=(shape(ROWS, COLS, dtype=F32), shape(ROWS, COLS, dtype=F32)),
            in_specs=[SMEM] + [VMEM] * 3,
            out_specs=(VMEM, VMEM),
            compiler_params=PARAMS,
            name="mix",
        )(place, att, wo_here, x)
        outputs.append((own_sum + swap(other_sum)).astype(BF16))

    new_cache = cache_here
    for moment in range(NCH):
        is_owner = owner[moment, 0] == shard_id
        updated = lax.dynamic_update_slice(new_cache, fresh_all[moment], (0, 0, filled, 0))
        new_cache = jnp.where(is_owner, updated, new_cache)
        filled = filled + jnp.where(is_owner, SPAN, 0).astype(jnp.int32)
    return (jnp.stack(outputs)[:, None], new_cache[None])


def solution(mesh):
    in_specs = (
        P("section", "tp", "kvp"),
        P(None, "tp", "kvp"),
        P("section", None),
        P("section", None, "tp", "kvp"),
        P("section", None, "tp", "kvp"),
        P("section", "tp", "kvp"),
        P("section", None, "tp", "kvp", None),
        P("section", "kvp"),
        P(None, "section"),
    )
    out_specs = (P(None, "section", "tp", "kvp"), P("section", None, "tp", "kvp", None))
    return jax.shard_map(body, mesh=mesh, in_specs=in_specs, out_specs=out_specs, check_vma=False)
```

```python
import functools
import math

import jax
import jax.numpy as jnp
from jax import lax
from jax.experimental import pallas as pl
from jax.experimental.pallas import tpu as pltpu
from jax.sharding import PartitionSpec as P

HD = 128
NCH = 2
EPS = 1e-05
N = 16
RING = 8
ROWS = 64
SPAN = 128
PRE = 256
D = 4096
COLS = 256
SCALE = 1.0 / math.sqrt(HD)
LOW = -1e30
F32 = jnp.float32
BF16 = jnp.bfloat16
RINGS = [list(range(RING)), list(range(RING, N))]
VMEM = pl.BlockSpec(memory_space=pltpu.VMEM)
SMEM = pl.BlockSpec(memory_space=pltpu.SMEM)
PARAMS = pltpu.CompilerParams(vmem_limit_bytes=40 * 1024 * 1024)


def dot(a, b):
    return jnp.dot(a, b, preferred_element_type=F32)


def dot_t(a, b):
    return lax.dot_general(a, b, (((1,), (1,)), ((), ())), preferred_element_type=F32)


def normalise(place, mine, other, gain, normed):
    t = place[0]
    for half, ref in ((t, mine), (1 - t, other)):
        total = jnp.zeros((ROWS, COLS), F32)
        for j in range(N):
            part = ref[j].astype(F32)
            total = total + part * part
        inverse = lax.rsqrt(jnp.sum(total, axis=1, keepdims=True) / D + EPS)
        rows = pl.ds(pl.multiple_of(half * ROWS, ROWS), ROWS)
        for j in range(N):
            cols = slice(j * COLS, (j + 1) * COLS)
            normed[rows, cols] = (ref[j].astype(F32) * inverse * gain[:, cols]).astype(BF16)


def project_first(place, lens, mine, other, gain, wq, wkv, q_out, kv_out, normed):
    normalise(place, mine, other, gain, normed)
    q_out[...] = dot(normed[...], wq[...]).astype(BF16)
    kv = dot_t(wkv[...], normed[...]).astype(BF16)
    filled = jnp.full((16, SPAN), lens[0].astype(F32), F32).astype(BF16)
    for j in range(N):
        kv_out[j, 0:32] = kv
        kv_out[j, 32:48] = filled


def project_later(place, mine, other, gain, wq, wkv_hbm, q_out, kv_out, normed, wkv, sem):
    copy = pltpu.make_async_copy(wkv_hbm, wkv, sem)
    copy.start()
    normalise(place, mine, other, gain, normed)
    q_out[...] = dot(normed[...], wq[...]).astype(BF16)
    copy.wait()
    kv_out[...] = dot_t(normed[...], wkv[...]).astype(BF16)


def attend(place, q_ref, held, first, *rest, later):
    if later:
        second, out, scores = rest
    else:
        out, scores = rest
    g = place[1]
    q = q_ref[...]
    slot = lax.broadcasted_iota(jnp.int32, (1, PRE), 1).astype(F32)
    top = jnp.full((SPAN, PRE), LOW, F32)
    for k in range(RING):
        for o in range(2):
            shard = (g if o == 0 else 1 - g) * RING + k
            filled = first[shard, 32:48][0:1].astype(F32)
            filled = jnp.concatenate([filled, filled], axis=1)
            s = dot_t(q, held[k, o, 0]) * SCALE
            s = jnp.where(slot < filled, s, LOW)
            b = (k * 2 + o) * PRE
            scores[:, b : b + PRE] = s
            top = jnp.maximum(top, s)
    top = jnp.max(top, axis=1, keepdims=True)
    row = lax.broadcasted_iota(jnp.int32, (SPAN, SPAN), 0)
    col = lax.broadcasted_iota(jnp.int32, (SPAN, SPAN), 1)
    keys = jnp.concatenate([first[g * RING + i, 0:32] for i in range(4)], axis=0)
    values = jnp.concatenate([first[g * RING + 4 + i, 0:32] for i in range(4)], axis=0)
    fresh = [dot(q, keys) * SCALE]
    if later:
        fresh.append(dot_t(q, second[:, 0:HD]) * SCALE)
    fresh[-1] = jnp.where(col <= row, fresh[-1], LOW)
    for s in fresh:
        top = jnp.maximum(top, jnp.max(s, axis=1, keepdims=True))
    total = jnp.zeros((SPAN, PRE), F32)
    acc = jnp.zeros((SPAN, HD), F32)
    for k in range(RING):
        for o in range(2):
            b = (k * 2 + o) * PRE
            e = jnp.exp(scores[:, b : b + PRE] - top)
            total = total + e
            acc = acc + dot(e.astype(BF16), held[k, o, 1])
    total = jnp.sum(total, axis=1, keepdims=True)
    for i, s in enumerate(fresh):
        e = jnp.exp(s - top)
        total = total + jnp.sum(e, axis=1, keepdims=True)
        if i == 0:
            acc = acc + dot_t(e.astype(BF16), values)
        else:
            acc = acc + dot(e.astype(BF16), second[:, HD : 2 * HD])
    result = (acc / total).astype(BF16)
    for j in range(N):
        out[j] = result


def mix(place, att, wo, x_ref, mine, other):
    t = place[0]
    acc = jnp.zeros((SPAN, COLS), F32)
    for j in range(N):
        acc = acc + dot(att[j], wo[j * HD : (j + 1) * HD, :])
    top, bottom = acc[0:ROWS], acc[ROWS:SPAN]
    mine[...] = x_ref[...].astype(F32) + jnp.where(t == 0, top, bottom)
    other[...] = jnp.where(t == 0, bottom, top)


def spread(block):
    return lax.all_to_all(block, "kvp", 0, 0, tiled=True)


def swap(block):
    return lax.ppermute(block, "tp", [(0, 1), (1, 0)])


def onward(block, cross):
    route = [(i, (i ^ cross) + 2) for i in range(30)]
    return lax.ppermute(block, ("section", "tp"), route)


def shape(*dims, dtype=BF16):
    return jax.ShapeDtypeStruct(dims, dtype)


def body(entering, feed, gain, wq, wkv, wo, cache, prefix_len, owner):
    shard_id = lax.axis_index("kvp")
    section_id = lax.axis_index("section")
    g = shard_id // RING
    place = jnp.stack([lax.axis_index("tp"), g]).astype(jnp.int32)
    filled = prefix_len[0, 0]
    wq_here, wkv_here, wo_here = wq[0, :, 0, :], wkv[0, :, 0, :], wo[0]
    cache_here = cache[0]

    prefix = cache_here[:, :, :PRE, :]
    own = lax.dynamic_index_in_dim(prefix, g, 1, False)
    give = lax.dynamic_index_in_dim(prefix, 1 - g, 1, False)
    got = lax.ppermute(give, "kvp", [(i, (i + RING) % N) for i in range(N)])
    held = lax.all_gather(jnp.stack([own, got]), "kvp", axis_index_groups=RINGS)

    wkv_t = wkv_here.T

    sums, fresh_all = [], []
    x = entering[0]
    for moment in range(NCH):
        if moment:
            passed = (onward(own_sum, 0) + onward(other_sum, 1)).astype(BF16)
            x = jnp.where(section_id == 0, feed[moment - 1], passed)
        mine = spread(jnp.broadcast_to(x[None], (N, ROWS, COLS)))
        other = swap(mine)
        scratch = [pltpu.VMEM((SPAN, D), BF16)]
        if moment == 0:
            q, kv = pl.pallas_call(
                project_first,
                out_shape=(shape(SPAN, HD), shape(N, 48, SPAN)),
                in_specs=[SMEM, SMEM] + [VMEM] * 5,
                out_specs=(VMEM, VMEM),
                scratch_shapes=scratch,
                compiler_params=PARAMS,
                name="project_first",
            )(place, filled[None], mine, other, gain, wq_here, wkv_t)
            first = spread(kv)
            wkv_late, first = lax.optimization_barrier((wkv_t, first))
            wkv_all = lax.all_gather(wkv_late, "kvp", axis_index_groups=RINGS)
            wkv_all = wkv_all.reshape(2 * HD, D)
            extra = (first,)
            both = jnp.transpose(first[:, 0:32].reshape(2, 2, HD, SPAN), (1, 0, 3, 2))
        else:
            q, kv = pl.pallas_call(
                project_later,
                out_shape=(shape(SPAN, HD), shape(SPAN, 2 * HD)),
                in_specs=[SMEM] + [VMEM] * 4 + [pl.BlockSpec(memory_space=pl.ANY)],
                out_specs=(VMEM, VMEM),
                scratch_shapes=scratch + [pltpu.VMEM((2 * HD, D), BF16), pltpu.SemaphoreType.DMA],
                compiler_params=PARAMS,
                name="project_later",
            )(place, mine, other, gain, wq_here, wkv_all)
            extra = (first, kv)
            late, kv = lax.optimization_barrier((sums[0], kv))
            sums[0] = late
            pair = lax.ppermute(kv, "kvp", [(i, (i + RING) % N) for i in range(N)])
            heads = jnp.where(g == 0, jnp.stack([kv, pair]), jnp.stack([pair, kv]))
            both = jnp.transpose(heads.reshape(2, SPAN, 2, HD), (2, 0, 1, 3))
        fresh_all.append(both)
        att = pl.pallas_call(
            functools.partial(attend, later=moment > 0),
            out_shape=shape(N, SPAN, HD),
            in_specs=[SMEM] + [VMEM] * (2 + len(extra)),
            out_specs=VMEM,
            scratch_shapes=[pltpu.VMEM((SPAN, N * PRE), F32)],
            compiler_params=PARAMS,
            name="attend",
        )(place, q, held, *extra)
        att = spread(att)
        own_sum, other_sum = pl.pallas_call(
            mix,
            out_shape=(shape(ROWS, COLS, dtype=F32), shape(ROWS, COLS, dtype=F32)),
            in_specs=[SMEM] + [VMEM] * 3,
            out_specs=(VMEM, VMEM),
            compiler_params=PARAMS,
            name="mix",
        )(place, att, wo_here, x)
        sums.append((own_sum, other_sum))

    outputs = [(own + swap(other)).astype(BF16) for own, other in sums]
    new_cache = cache_here
    for moment in range(NCH):
        is_owner = owner[moment, 0] == shard_id
        updated = lax.dynamic_update_slice(new_cache, fresh_all[moment], (0, 0, filled, 0))
        new_cache = jnp.where(is_owner, updated, new_cache)
        filled = filled + jnp.where(is_owner, SPAN, 0).astype(jnp.int32)
    return (jnp.stack(outputs)[:, None], new_cache[None])


def solution(mesh):
    in_specs = (
        P("section", "tp", "kvp"),
        P(None, "tp", "kvp"),
        P("section", None),
        P("section", None, "tp", "kvp"),
        P("section", None, "tp", "kvp"),
        P("section", "tp", "kvp"),
        P("section", None, "tp", "kvp", None),
        P("section", "kvp"),
        P(None, "section"),
    )
    out_specs = (P(None, "section", "tp", "kvp"), P("section", None, "tp", "kvp", None))
    return jax.shard_map(body, mesh=mesh, in_specs=in_specs, out_specs=out_specs, check_vma=False)
```

```python
import functools
import math

import jax
import jax.numpy as jnp
from jax import lax
from jax.experimental import pallas as pl
from jax.experimental.pallas import tpu as pltpu
from jax.sharding import PartitionSpec as P

HD = 128
NCH = 2
EPS = 1e-05
N = 16
RING = 8
ROWS = 64
SPAN = 128
PRE = 256
D = 4096
COLS = 256
SCALE = 1.0 / math.sqrt(HD)
LOW = -1e30
F32 = jnp.float32
BF16 = jnp.bfloat16
RINGS = [list(range(RING)), list(range(RING, N))]
VMEM = pl.BlockSpec(memory_space=pltpu.VMEM)
SMEM = pl.BlockSpec(memory_space=pltpu.SMEM)
PARAMS = pltpu.CompilerParams(vmem_limit_bytes=24 * 1024 * 1024)


def dot(a, b):
    return jnp.dot(a, b, preferred_element_type=F32)


def dot_t(a, b):
    return lax.dot_general(a, b, (((1,), (1,)), ((), ())), preferred_element_type=F32)


def normalise(ref, gain, normed, rows):
    total = jnp.zeros((ROWS, COLS), F32)
    for j in range(N):
        part = ref[j].astype(F32)
        total = total + part * part
    inverse = lax.rsqrt(jnp.sum(total, axis=1, keepdims=True) / D + EPS)
    for j in range(N):
        cols = slice(j * COLS, (j + 1) * COLS)
        normed[rows, cols] = (ref[j].astype(F32) * inverse * gain[:, cols]).astype(BF16)


def half_rows(half):
    return pl.ds(pl.multiple_of(half * ROWS, ROWS), ROWS)


def project_first(place, lens, mine, other, gain, wq, wkv, q_out, kv_out, normed):
    t = place[0]
    normalise(mine, gain, normed, half_rows(t))
    normalise(other, gain, normed, half_rows(1 - t))
    q_out[...] = dot(normed[...], wq[...]).astype(BF16)
    kv = dot_t(wkv[...], normed[...]).astype(BF16)
    filled = jnp.full((16, SPAN), lens[0].astype(F32), F32).astype(BF16)
    for j in range(N):
        kv_out[j, 0:32] = kv
        kv_out[j, 32:48] = filled


def over_prefixes(g, q, held, first, scores):
    count = q.shape[0]
    slot = lax.broadcasted_iota(jnp.int32, (1, PRE), 1).astype(F32)
    top = jnp.full((count, PRE), LOW, F32)
    for k in range(RING):
        for o in range(2):
            shard = (g if o == 0 else 1 - g) * RING + k
            filled = first[shard, 32:48][0:1].astype(F32)
            filled = jnp.concatenate([filled, filled], axis=1)
            s = dot_t(q, held[k, o, 0]) * SCALE
            s = jnp.where(slot < filled, s, LOW)
            b = (k * 2 + o) * PRE
            scores[:, b : b + PRE] = s
            top = jnp.maximum(top, s)
    top = jnp.max(top, axis=1, keepdims=True)
    total = jnp.zeros((count, PRE), F32)
    acc = jnp.zeros((count, HD), F32)
    for k in range(RING):
        for o in range(2):
            b = (k * 2 + o) * PRE
            e = jnp.exp(scores[:, b : b + PRE] - top)
            total = total + e
            acc = acc + dot(e.astype(BF16), held[k, o, 1])
    return top, jnp.sum(total, axis=1, keepdims=True), acc


def with_spans(start, top, total, acc, spans):
    count = acc.shape[0]
    row = lax.broadcasted_iota(jnp.int32, (count, SPAN), 0) + start
    col = lax.broadcasted_iota(jnp.int32, (count, SPAN), 1)
    spans = list(spans)
    spans[-1] = (jnp.where(col <= row, spans[-1][0], LOW), spans[-1][1])
    peak = top
    for s, _ in spans:
        peak = jnp.maximum(peak, jnp.max(s, axis=1, keepdims=True))
    weight = jnp.exp(top - peak)
    total = total * weight
    acc = acc * weight
    for s, product in spans:
        e = jnp.exp(s - peak)
        total = total + jnp.sum(e, axis=1, keepdims=True)
        acc = acc + product(e.astype(BF16))
    return (acc / total).astype(BF16)


def first_span(g, q, first):
    keys = jnp.concatenate([first[g * RING + i, 0:32] for i in range(4)], axis=0)
    values = jnp.concatenate([first[g * RING + 4 + i, 0:32] for i in range(4)], axis=0)
    return dot(q, keys) * SCALE, lambda e: dot_t(e, values)


def attend_first(place, q_ref, held, first, out, scores):
    g = place[1]
    q = q_ref[...]
    top, total, acc = over_prefixes(g, q, held, first, scores)
    result = with_spans(0, top, total, acc, [first_span(g, q, first)])
    for j in range(N):
        out[j] = result


def own_rows(place, x, gain, wq, held, first, normed, q_out, top_out, sum_out, acc_out, scores):
    normalise(x, gain, normed, slice(0, ROWS))
    q = dot(normed[...], wq[...]).astype(BF16)
    q_out[...] = q
    top, total, acc = over_prefixes(place[1], q, held, first, scores)
    top_out[...] = jnp.broadcast_to(top, (ROWS, HD))
    sum_out[...] = jnp.broadcast_to(total, (ROWS, HD))
    acc_out[...] = acc


def other_rows(
    place, x, gain, wq, wkv, held, first, normed_own, q_own, top_own, sum_own, acc_own, out, kv, normed, scores
):
    t, g = place[0], place[1]
    normalise(x, gain, normed, slice(0, ROWS))
    q = dot(normed[...], wq[...]).astype(BF16)
    kv[half_rows(1 - t), :] = dot_t(normed[...], wkv[...]).astype(BF16)
    kv[half_rows(t), :] = dot_t(normed_own[...], wkv[...]).astype(BF16)
    top, total, acc = over_prefixes(g, q, held, first, scores)
    keys, values = kv[:, 0:HD], kv[:, HD : 2 * HD]
    parts = (
        (t, q_own[...], top_own[:, 0:1], sum_own[:, 0:1], acc_own[...]),
        (1 - t, q, top, total, acc),
    )
    for half, q, top, total, acc in parts:
        spans = [first_span(g, q, first), (dot_t(q, keys) * SCALE, lambda e: dot(e, values))]
        result = with_spans(half * ROWS, top, total, acc, spans)
        for j in range(N):
            out[j, half_rows(half), :] = result


def mix(place, att, wo, x_ref, mine, other):
    t = place[0]
    acc = jnp.zeros((SPAN, COLS), F32)
    for j in range(N):
        acc = acc + dot(att[j], wo[j * HD : (j + 1) * HD, :])
    top, bottom = acc[0:ROWS], acc[ROWS:SPAN]
    mine[...] = x_ref[...].astype(F32) + jnp.where(t == 0, top, bottom)
    other[...] = jnp.where(t == 0, bottom, top)


def spread(block):
    return lax.all_to_all(block, "kvp", 0, 0, tiled=True)


def swap(block):
    return lax.ppermute(block, "tp", [(0, 1), (1, 0)])


def onward(block, cross):
    route = [(i, (i ^ cross) + 2) for i in range(30)]
    return lax.ppermute(block, ("section", "tp"), route)


def shape(*dims, dtype=BF16):
    return jax.ShapeDtypeStruct(dims, dtype)


def body(entering, feed, gain, wq, wkv, wo, cache, prefix_len, owner):
    shard_id = lax.axis_index("kvp")
    section_id = lax.axis_index("section")
    g = shard_id // RING
    place = jnp.stack([lax.axis_index("tp"), g]).astype(jnp.int32)
    filled = prefix_len[0, 0]
    wq_here, wkv_here, wo_here = wq[0, :, 0, :], wkv[0, :, 0, :], wo[0]
    cache_here = cache[0]

    prefix = cache_here[:, :, :PRE, :]
    own = lax.dynamic_index_in_dim(prefix, g, 1, False)
    give = lax.dynamic_index_in_dim(prefix, 1 - g, 1, False)
    got = lax.ppermute(give, "kvp", [(i, (i + RING) % N) for i in range(N)])
    held = lax.all_gather(jnp.stack([own, got]), "kvp", axis_index_groups=RINGS)

    wkv_t = wkv_here.T

    def updated(cache_now, fresh, moment):
        start = filled
        for u in range(moment):
            start = start + jnp.where(owner[u, 0] == shard_id, SPAN, 0).astype(jnp.int32)
        changed = lax.dynamic_update_slice(cache_now, fresh, (0, 0, start, 0))
        return jnp.where(owner[moment, 0] == shard_id, changed, cache_now)

    sums, fresh_all = [], []
    x = entering[0]
    for moment in range(NCH):
        if moment:
            passed = (onward(own_sum, 0) + onward(other_sum, 1)).astype(BF16)
            x = jnp.where(section_id == 0, feed[moment - 1], passed)
        mine = spread(jnp.broadcast_to(x[None], (N, ROWS, COLS)))
        other = swap(mine)
        if moment == 0:
            q, kv = pl.pallas_call(
                project_first,
                out_shape=(shape(SPAN, HD), shape(N, 48, SPAN)),
                in_specs=[SMEM, SMEM] + [VMEM] * 5,
                out_specs=(VMEM, VMEM),
                scratch_shapes=[pltpu.VMEM((SPAN, D), BF16)],
                compiler_params=PARAMS,
                name="project_first",
            )(place, filled[None], mine, other, gain, wq_here, wkv_t)
            first = spread(kv)
            wkv_late, first = lax.optimization_barrier((wkv_t, first))
            wkv_all = lax.all_gather(wkv_late, "kvp", axis_index_groups=RINGS)
            wkv_all = wkv_all.reshape(2 * HD, D)
            both = jnp.transpose(first[:, 0:32].reshape(2, 2, HD, SPAN), (1, 0, 3, 2))
            fresh_all.append(both)
            att = pl.pallas_call(
                attend_first,
                out_shape=shape(N, SPAN, HD),
                in_specs=[SMEM] + [VMEM] * 3,
                out_specs=VMEM,
                scratch_shapes=[pltpu.VMEM((SPAN, N * PRE), F32)],
                compiler_params=PARAMS,
                name="attend_first",
            )(place, q, held, first)
        else:
            mine, wkv_all = lax.optimization_barrier((mine, wkv_all))
            own_state = pl.pallas_call(
                own_rows,
                out_shape=(shape(ROWS, D), shape(ROWS, HD)) + (shape(ROWS, HD, dtype=F32),) * 3,
                in_specs=[SMEM] + [VMEM] * 5,
                out_specs=(VMEM,) * 5,
                scratch_shapes=[pltpu.VMEM((ROWS, N * PRE), F32)],
                compiler_params=PARAMS,
                name="own_rows",
            )(place, mine, gain, wq_here, held, first)
            att, kv = pl.pallas_call(
                other_rows,
                out_shape=(shape(N, SPAN, HD), shape(SPAN, 2 * HD)),
                in_specs=[SMEM] + [VMEM] * 11,
                out_specs=(VMEM, VMEM),
                scratch_shapes=[pltpu.VMEM((ROWS, D), BF16), pltpu.VMEM((ROWS, N * PRE), F32)],
                compiler_params=PARAMS,
                name="other_rows",
            )(place, other, gain, wq_here, wkv_all, held, first, *own_state)
            late, kv = lax.optimization_barrier((sums[0], kv))
            sums[0] = late
            pair = lax.ppermute(kv, "kvp", [(i, (i + RING) % N) for i in range(N)])
            heads = jnp.where(g == 0, jnp.stack([kv, pair]), jnp.stack([pair, kv]))
            both = jnp.transpose(heads.reshape(2, SPAN, 2, HD), (2, 0, 1, 3))
            fresh_all.append(both)
        att = spread(att)
        if moment:
            new_cache = cache_here
            for u in range(NCH):
                new_cache = updated(new_cache, fresh_all[u], u)
            new_cache, att = lax.optimization_barrier((new_cache, att))
        own_sum, other_sum = pl.pallas_call(
            mix,
            out_shape=(shape(ROWS, COLS, dtype=F32), shape(ROWS, COLS, dtype=F32)),
            in_specs=[SMEM] + [VMEM] * 3,
            out_specs=(VMEM, VMEM),
            compiler_params=PARAMS,
            name="mix",
        )(place, att, wo_here, x)
        sums.append((own_sum, other_sum))
    outputs = [(mine + swap(other)).astype(BF16) for mine, other in sums]
    return (jnp.stack(outputs)[:, None], new_cache[None])


def solution(mesh):
    in_specs = (
        P("section", "tp", "kvp"),
        P(None, "tp", "kvp"),
        P("section", None),
        P("section", None, "tp", "kvp"),
        P("section", None, "tp", "kvp"),
        P("section", "tp", "kvp"),
        P("section", None, "tp", "kvp", None),
        P("section", "kvp"),
        P(None, "section"),
    )
    out_specs = (P(None, "section", "tp", "kvp"), P("section", None, "tp", "kvp", None))
    return jax.shard_map(body, mesh=mesh, in_specs=in_specs, out_specs=out_specs, check_vma=False)
```

```python
import functools
import math

import jax
import jax.numpy as jnp
from jax import lax
from jax.experimental import pallas as pl
from jax.experimental.pallas import tpu as pltpu
from jax.sharding import PartitionSpec as P

HD = 128
NCH = 2
EPS = 1e-05
N = 16
RING = 8
ROWS = 64
SPAN = 128
PRE = 256
D = 4096
COLS = 256
SCALE = 1.0 / math.sqrt(HD)
LOW = -1e30
F32 = jnp.float32
BF16 = jnp.bfloat16
RINGS = [list(range(RING)), list(range(RING, N))]
VMEM = pl.BlockSpec(memory_space=pltpu.VMEM)
SMEM = pl.BlockSpec(memory_space=pltpu.SMEM)
PARAMS = pltpu.CompilerParams(vmem_limit_bytes=40 * 1024 * 1024)


def dot(a, b):
    return jnp.dot(a, b, preferred_element_type=F32)


def dot_t(a, b):
    return lax.dot_general(a, b, (((1,), (1,)), ((), ())), preferred_element_type=F32)


def normalise(ref, gain, normed, rows):
    total = jnp.zeros((ROWS, COLS), F32)
    for j in range(N):
        part = ref[j].astype(F32)
        total = total + part * part
    inverse = lax.rsqrt(jnp.sum(total, axis=1, keepdims=True) / D + EPS)
    for j in range(N):
        cols = slice(j * COLS, (j + 1) * COLS)
        normed[rows, cols] = (ref[j].astype(F32) * inverse * gain[:, cols]).astype(BF16)


def half_rows(half):
    return pl.ds(pl.multiple_of(half * ROWS, ROWS), ROWS)


def project_first(place, lens, mine, other, gain, wq, wkv, q_out, kv_out, normed):
    t = place[0]
    normalise(mine, gain, normed, half_rows(t))
    normalise(other, gain, normed, half_rows(1 - t))
    q_out[...] = dot(normed[...], wq[...]).astype(BF16)
    kv = dot_t(wkv[...], normed[...]).astype(BF16)
    filled = jnp.full((16, SPAN), lens[0].astype(F32), F32).astype(BF16)
    for j in range(N):
        kv_out[j, 0:32] = kv
        kv_out[j, 32:48] = filled


def over_prefixes(g, q, held, first, scores):
    count = q.shape[0]
    slot = lax.broadcasted_iota(jnp.int32, (1, PRE), 1).astype(F32)
    top = jnp.full((count, PRE), LOW, F32)
    for k in range(RING):
        for o in range(2):
            shard = (g if o == 0 else 1 - g) * RING + k
            filled = first[shard, 32:48][0:1].astype(F32)
            filled = jnp.concatenate([filled, filled], axis=1)
            s = dot_t(q, held[k, o, 0]) * SCALE
            s = jnp.where(slot < filled, s, LOW)
            b = (k * 2 + o) * PRE
            scores[:, b : b + PRE] = s
            top = jnp.maximum(top, s)
    top = jnp.max(top, axis=1, keepdims=True)
    total = jnp.zeros((count, PRE), F32)
    acc = jnp.zeros((count, HD), F32)
    for k in range(RING):
        for o in range(2):
            b = (k * 2 + o) * PRE
            e = jnp.exp(scores[:, b : b + PRE] - top)
            total = total + e
            acc = acc + dot(e.astype(BF16), held[k, o, 1])
    return top, jnp.sum(total, axis=1, keepdims=True), acc


def with_spans(start, top, total, acc, spans):
    count = acc.shape[0]
    row = lax.broadcasted_iota(jnp.int32, (count, SPAN), 0) + start
    col = lax.broadcasted_iota(jnp.int32, (count, SPAN), 1)
    spans = list(spans)
    spans[-1] = (jnp.where(col <= row, spans[-1][0], LOW), spans[-1][1])
    peak = top
    for s, _ in spans:
        peak = jnp.maximum(peak, jnp.max(s, axis=1, keepdims=True))
    weight = jnp.exp(top - peak)
    total = total * weight
    acc = acc * weight
    for s, product in spans:
        e = jnp.exp(s - peak)
        total = total + jnp.sum(e, axis=1, keepdims=True)
        acc = acc + product(e.astype(BF16))
    return (acc / total).astype(BF16)


def first_span(g, q, first):
    keys = jnp.concatenate([first[g * RING + i, 0:32] for i in range(4)], axis=0)
    values = jnp.concatenate([first[g * RING + 4 + i, 0:32] for i in range(4)], axis=0)
    return dot(q, keys) * SCALE, lambda e: dot_t(e, values)


def attend_first(place, q_ref, held, first, out, scores):
    g = place[1]
    q = q_ref[...]
    top, total, acc = over_prefixes(g, q, held, first, scores)
    result = with_spans(0, top, total, acc, [first_span(g, q, first)])
    for j in range(N):
        out[j] = result


def own_rows(place, x, gain, wq, held, first, normed, q_out, top_out, sum_out, acc_out, scores):
    normalise(x, gain, normed, slice(0, ROWS))
    q = dot(normed[...], wq[...]).astype(BF16)
    q_out[...] = q
    top, total, acc = over_prefixes(place[1], q, held, first, scores)
    top_out[...] = jnp.broadcast_to(top, (ROWS, HD))
    sum_out[...] = jnp.broadcast_to(total, (ROWS, HD))
    acc_out[...] = acc


def other_rows(
    place, x, gain, wq, wkv, held, first, normed_own, q_own, top_own, sum_own, acc_own, out, kv, normed, scores
):
    t, g = place[0], place[1]
    normalise(x, gain, normed, slice(0, ROWS))
    q = dot(normed[...], wq[...]).astype(BF16)
    both = jnp.concatenate([normed_own[...], normed[...]], axis=0)
    both = dot_t(both, wkv[...]).astype(BF16)
    kv[half_rows(t), :] = both[0:ROWS]
    kv[half_rows(1 - t), :] = both[ROWS:SPAN]
    top, total, acc = over_prefixes(g, q, held, first, scores)
    keys, values = kv[:, 0:HD], kv[:, HD : 2 * HD]
    parts = (
        (t, q_own[...], top_own[:, 0:1], sum_own[:, 0:1], acc_own[...]),
        (1 - t, q, top, total, acc),
    )
    for half, q, top, total, acc in parts:
        spans = [first_span(g, q, first), (dot_t(q, keys) * SCALE, lambda e: dot(e, values))]
        result = with_spans(half * ROWS, top, total, acc, spans)
        for j in range(N):
            out[j, half_rows(half), :] = result


def mix(place, att, wo, x_ref, mine, other):
    t = place[0]
    acc = jnp.zeros((SPAN, COLS), F32)
    for j in range(N):
        acc = acc + dot(att[j], wo[j * HD : (j + 1) * HD, :])
    top, bottom = acc[0:ROWS], acc[ROWS:SPAN]
    mine[...] = x_ref[...].astype(F32) + jnp.where(t == 0, top, bottom)
    other[...] = jnp.where(t == 0, bottom, top)


def spread(block):
    return lax.all_to_all(block, "kvp", 0, 0, tiled=True)


def swap(block):
    return lax.ppermute(block, "tp", [(0, 1), (1, 0)])


def onward(block, cross):
    route = [(i, (i ^ cross) + 2) for i in range(30)]
    return lax.ppermute(block, ("section", "tp"), route)


def shape(*dims, dtype=BF16):
    return jax.ShapeDtypeStruct(dims, dtype)


def body(entering, feed, gain, wq, wkv, wo, cache, prefix_len, owner):
    shard_id = lax.axis_index("kvp")
    section_id = lax.axis_index("section")
    g = shard_id // RING
    place = jnp.stack([lax.axis_index("tp"), g]).astype(jnp.int32)
    filled = prefix_len[0, 0]
    wq_here, wkv_here, wo_here = wq[0, :, 0, :], wkv[0, :, 0, :], wo[0]
    cache_here = cache[0]

    prefix = cache_here[:, :, :PRE, :]
    own = lax.dynamic_index_in_dim(prefix, g, 1, False)
    give = lax.dynamic_index_in_dim(prefix, 1 - g, 1, False)
    got = lax.ppermute(give, "kvp", [(i, (i + RING) % N) for i in range(N)])
    held = lax.all_gather(jnp.stack([own, got]), "kvp", axis_index_groups=RINGS)

    wkv_t = wkv_here.T

    def updated(cache_now, fresh, moment):
        start = filled
        for u in range(moment):
            start = start + jnp.where(owner[u, 0] == shard_id, SPAN, 0).astype(jnp.int32)
        changed = lax.dynamic_update_slice(cache_now, fresh, (0, 0, start, 0))
        return jnp.where(owner[moment, 0] == shard_id, changed, cache_now)

    sums, fresh_all = [], []
    x = entering[0]
    for moment in range(NCH):
        if moment:
            passed = (onward(own_sum, 0) + onward(other_sum, 1)).astype(BF16)
            x = jnp.where(section_id == 0, feed[moment - 1], passed)
        mine = spread(jnp.broadcast_to(x[None], (N, ROWS, COLS)))
        other = swap(mine)
        if moment == 0:
            q, kv = pl.pallas_call(
                project_first,
                out_shape=(shape(SPAN, HD), shape(N, 48, SPAN)),
                in_specs=[SMEM, SMEM] + [VMEM] * 5,
                out_specs=(VMEM, VMEM),
                scratch_shapes=[pltpu.VMEM((SPAN, D), BF16)],
                compiler_params=PARAMS,
                name="project_first",
            )(place, filled[None], mine, other, gain, wq_here, wkv_t)
            first = spread(kv)
            wkv_late, first = lax.optimization_barrier((wkv_t, first))
            wkv_all = lax.all_gather(wkv_late, "kvp", axis_index_groups=RINGS)
            wkv_all = wkv_all.reshape(2 * HD, D)
            both = jnp.transpose(first[:, 0:32].reshape(2, 2, HD, SPAN), (1, 0, 3, 2))
            fresh_all.append(both)
            att = pl.pallas_call(
                attend_first,
                out_shape=shape(N, SPAN, HD),
                in_specs=[SMEM] + [VMEM] * 3,
                out_specs=VMEM,
                scratch_shapes=[pltpu.VMEM((SPAN, N * PRE), F32)],
                compiler_params=PARAMS,
                name="attend_first",
            )(place, q, held, first)
        else:
            mine, wkv_all = lax.optimization_barrier((mine, wkv_all))
            own_state = pl.pallas_call(
                own_rows,
                out_shape=(shape(ROWS, D), shape(ROWS, HD)) + (shape(ROWS, HD, dtype=F32),) * 3,
                in_specs=[SMEM] + [VMEM] * 5,
                out_specs=(VMEM,) * 5,
                scratch_shapes=[pltpu.VMEM((ROWS, N * PRE), F32)],
                compiler_params=PARAMS,
                name="own_rows",
            )(place, mine, gain, wq_here, held, first)
            att, kv = pl.pallas_call(
                other_rows,
                out_shape=(shape(N, SPAN, HD), shape(SPAN, 2 * HD)),
                in_specs=[SMEM] + [VMEM] * 11,
                out_specs=(VMEM, VMEM),
                scratch_shapes=[pltpu.VMEM((ROWS, D), BF16), pltpu.VMEM((ROWS, N * PRE), F32)],
                compiler_params=PARAMS,
                name="other_rows",
            )(place, other, gain, wq_here, wkv_all, held, first, *own_state)
            late, kv = lax.optimization_barrier((sums[0], kv))
            sums[0] = late
            pair = lax.ppermute(kv, "kvp", [(i, (i + RING) % N) for i in range(N)])
            heads = jnp.where(g == 0, jnp.stack([kv, pair]), jnp.stack([pair, kv]))
            both = jnp.transpose(heads.reshape(2, SPAN, 2, HD), (2, 0, 1, 3))
            fresh_all.append(both)
        att = spread(att)
        if moment:
            new_cache = cache_here
            for u in range(NCH):
                new_cache = updated(new_cache, fresh_all[u], u)
            new_cache, att = lax.optimization_barrier((new_cache, att))
        own_sum, other_sum = pl.pallas_call(
            mix,
            out_shape=(shape(ROWS, COLS, dtype=F32), shape(ROWS, COLS, dtype=F32)),
            in_specs=[SMEM] + [VMEM] * 3,
            out_specs=(VMEM, VMEM),
            compiler_params=PARAMS,
            name="mix",
        )(place, att, wo_here, x)
        sums.append((own_sum, other_sum))
    outputs = [(mine + swap(other)).astype(BF16) for mine, other in sums]
    return (jnp.stack(outputs)[:, None], new_cache[None])


def solution(mesh):
    in_specs = (
        P("section", "tp", "kvp"),
        P(None, "tp", "kvp"),
        P("section", None),
        P("section", None, "tp", "kvp"),
        P("section", None, "tp", "kvp"),
        P("section", "tp", "kvp"),
        P("section", None, "tp", "kvp", None),
        P("section", "kvp"),
        P(None, "section"),
    )
    out_specs = (P(None, "section", "tp", "kvp"), P("section", None, "tp", "kvp", None))
    return jax.shard_map(body, mesh=mesh, in_specs=in_specs, out_specs=out_specs, check_vma=False)
```

```python
import functools
import math

import jax
import jax.numpy as jnp
from jax import lax
from jax.experimental import pallas as pl
from jax.experimental.pallas import tpu as pltpu
from jax.sharding import PartitionSpec as P

HD = 128
NCH = 2
EPS = 1e-05
N = 16
RING = 8
ROWS = 64
SPAN = 128
PRE = 256
D = 4096
COLS = 256
SCALE = 1.0 / math.sqrt(HD)
LOW = -1e30
MARK = 1024.0
F32 = jnp.float32
BF16 = jnp.bfloat16
RINGS = [list(range(RING)), list(range(RING, N))]
VMEM = pl.BlockSpec(memory_space=pltpu.VMEM)
SMEM = pl.BlockSpec(memory_space=pltpu.SMEM)
PARAMS = pltpu.CompilerParams(vmem_limit_bytes=40 * 1024 * 1024)


def dot(a, b):
    return jnp.dot(a, b, preferred_element_type=F32)


def dot_t(a, b):
    return lax.dot_general(a, b, (((1,), (1,)), ((), ())), preferred_element_type=F32)


def normalise(ref, gain, normed, rows):
    total = jnp.zeros((ROWS, COLS), F32)
    for j in range(N):
        part = ref[j].astype(F32)
        total = total + part * part
    inverse = lax.rsqrt(jnp.sum(total, axis=1, keepdims=True) / D + EPS)
    for j in range(N):
        cols = slice(j * COLS, (j + 1) * COLS)
        normed[rows, cols] = (ref[j].astype(F32) * inverse * gain[:, cols]).astype(BF16)


def half_rows(half):
    return pl.ds(pl.multiple_of(half * ROWS, ROWS), ROWS)


def project_first(place, mine, other, gain, wq, wkv, q_out, kv_out, normed):
    t = place[0]
    normalise(mine, gain, normed, half_rows(t))
    normalise(other, gain, normed, half_rows(1 - t))
    q_out[...] = dot(normed[...], wq[...]).astype(BF16)
    kv = dot_t(wkv[...], normed[...]).astype(BF16)
    for j in range(RING):
        kv_out[j] = kv


def over_prefixes(q, held, scores):
    count = q.shape[0]
    slot = lax.broadcasted_iota(jnp.int32, (1, PRE), 1).astype(F32)
    top = jnp.full((count, PRE), LOW, F32)
    for k in range(RING):
        for o in range(2):
            mark = held[k, o, 0, PRE - 16 : PRE][15:16].astype(F32)
            filled = jnp.where(mark > MARK / 2, mark / MARK, float(PRE))
            filled = jnp.concatenate([filled, filled], axis=1)
            s = dot_t(q, held[k, o, 0]) * SCALE
            s = jnp.where(slot < filled, s, LOW)
            b = (k * 2 + o) * PRE
            scores[:, b : b + PRE] = s
            top = jnp.maximum(top, s)
    top = jnp.max(top, axis=1, keepdims=True)
    total = jnp.zeros((count, PRE), F32)
    acc = jnp.zeros((count, HD), F32)
    for k in range(RING):
        for o in range(2):
            b = (k * 2 + o) * PRE
            e = jnp.exp(scores[:, b : b + PRE] - top)
            total = total + e
            acc = acc + dot(e.astype(BF16), held[k, o, 1])
    return top, jnp.sum(total, axis=1, keepdims=True), acc


def with_spans(start, top, total, acc, spans):
    count = acc.shape[0]
    row = lax.broadcasted_iota(jnp.int32, (count, SPAN), 0) + start
    col = lax.broadcasted_iota(jnp.int32, (count, SPAN), 1)
    spans = list(spans)
    spans[-1] = (jnp.where(col <= row, spans[-1][0], LOW), spans[-1][1])
    peak = top
    for s, _ in spans:
        peak = jnp.maximum(peak, jnp.max(s, axis=1, keepdims=True))
    weight = jnp.exp(top - peak)
    total = total * weight
    acc = acc * weight
    for s, product in spans:
        e = jnp.exp(s - peak)
        total = total + jnp.sum(e, axis=1, keepdims=True)
        acc = acc + product(e.astype(BF16))
    return (acc / total).astype(BF16)


def first_span(q, first):
    keys = jnp.concatenate([first[i] for i in range(4)], axis=0)
    values = jnp.concatenate([first[4 + i] for i in range(4)], axis=0)
    return dot(q, keys) * SCALE, lambda e: dot_t(e, values)


def attend_first(place, q_ref, held, first, out, scores):
    g = place[1]
    q = q_ref[...]
    top, total, acc = over_prefixes(q, held, scores)
    result = with_spans(0, top, total, acc, [first_span(q, first)])
    for j in range(N):
        out[j] = result


def own_rows(place, x, gain, wq, held, first, normed, q_out, top_out, sum_out, acc_out, scores):
    normalise(x, gain, normed, slice(0, ROWS))
    q = dot(normed[...], wq[...]).astype(BF16)
    q_out[...] = q
    top, total, acc = over_prefixes(q, held, scores)
    top_out[...] = jnp.broadcast_to(top, (ROWS, HD))
    sum_out[...] = jnp.broadcast_to(total, (ROWS, HD))
    acc_out[...] = acc


def other_rows(
    place, x, gain, wq, wkv, held, first, normed_own, q_own, top_own, sum_own, acc_own, out, kv, normed, scores
):
    t, g = place[0], place[1]
    normalise(x, gain, normed, slice(0, ROWS))
    q = dot(normed[...], wq[...]).astype(BF16)
    both = jnp.concatenate([normed_own[...], normed[...]], axis=0)
    both = dot_t(both, wkv[...]).astype(BF16)
    kv[half_rows(t), :] = both[0:ROWS]
    kv[half_rows(1 - t), :] = both[ROWS:SPAN]
    top, total, acc = over_prefixes(q, held, scores)
    keys, values = kv[:, 0:HD], kv[:, HD : 2 * HD]
    parts = (
        (t, q_own[...], top_own[:, 0:1], sum_own[:, 0:1], acc_own[...]),
        (1 - t, q, top, total, acc),
    )
    for half, q, top, total, acc in parts:
        spans = [first_span(q, first), (dot_t(q, keys) * SCALE, lambda e: dot(e, values))]
        result = with_spans(half * ROWS, top, total, acc, spans)
        for j in range(N):
            out[j, half_rows(half), :] = result


def mix(place, att, wo, x_ref, mine, other):
    t = place[0]
    acc = jnp.zeros((SPAN, COLS), F32)
    for j in range(N):
        acc = acc + dot(att[j], wo[j * HD : (j + 1) * HD, :])
    top, bottom = acc[0:ROWS], acc[ROWS:SPAN]
    mine[...] = x_ref[...].astype(F32) + jnp.where(t == 0, top, bottom)
    other[...] = jnp.where(t == 0, bottom, top)


def spread(block):
    return lax.all_to_all(block, "kvp", 0, 0, tiled=True)


def swap(block):
    return lax.ppermute(block, "tp", [(0, 1), (1, 0)])


def onward(block, cross):
    route = [(i, (i ^ cross) + 2) for i in range(30)]
    return lax.ppermute(block, ("section", "tp"), route)


def shape(*dims, dtype=BF16):
    return jax.ShapeDtypeStruct(dims, dtype)


def body(entering, feed, gain, wq, wkv, wo, cache, prefix_len, owner):
    shard_id = lax.axis_index("kvp")
    section_id = lax.axis_index("section")
    g = shard_id // RING
    place = jnp.stack([lax.axis_index("tp"), g]).astype(jnp.int32)
    filled = prefix_len[0, 0]
    wq_here, wkv_here, wo_here = wq[0, :, 0, :], wkv[0, :, 0, :], wo[0]
    cache_here = cache[0]

    prefix = cache_here[:, :, :PRE, :]
    last = prefix[0:1, :, PRE - 1 : PRE]
    last = jnp.where(filled < PRE, (filled.astype(F32) * MARK).astype(BF16), last)
    prefix = lax.dynamic_update_slice(prefix, last, (0, 0, PRE - 1, 0))
    own = lax.dynamic_index_in_dim(prefix, g, 1, False)
    give = lax.dynamic_index_in_dim(prefix, 1 - g, 1, False)
    got = lax.ppermute(give, "kvp", [(i, (i + RING) % N) for i in range(N)])
    held = lax.all_gather(jnp.stack([own, got]), "kvp", axis_index_groups=RINGS)

    wkv_t = wkv_here.T

    def updated(cache_now, fresh, moment, owner):
        start = filled
        for u in range(moment):
            start = start + jnp.where(owner[u, 0] == shard_id, SPAN, 0).astype(jnp.int32)
        changed = lax.dynamic_update_slice(cache_now, fresh, (0, 0, start, 0))
        return jnp.where(owner[moment, 0] == shard_id, changed, cache_now)

    sums = []
    x = entering[0]
    for moment in range(NCH):
        if moment:
            passed = (onward(own_sum, 0) + onward(other_sum, 1)).astype(BF16)
            x = jnp.where(section_id == 0, feed[moment - 1], passed)
        mine = spread(jnp.broadcast_to(x[None], (N, ROWS, COLS)))
        other = swap(mine)
        if moment == 0:
            q, kv = pl.pallas_call(
                project_first,
                out_shape=(shape(SPAN, HD), shape(RING, 32, SPAN)),
                in_specs=[SMEM] + [VMEM] * 5,
                out_specs=(VMEM, VMEM),
                scratch_shapes=[pltpu.VMEM((SPAN, D), BF16)],
                compiler_params=PARAMS,
                name="project_first",
            )(place, mine, other, gain, wq_here, wkv_t)
            first = lax.all_to_all(kv, "kvp", 0, 0, tiled=True, axis_index_groups=RINGS)
            wkv_late, first = lax.optimization_barrier((wkv_t, first))
            wkv_all = lax.all_gather(wkv_late, "kvp", axis_index_groups=RINGS)
            wkv_all = wkv_all.reshape(2 * HD, D)
            kv_first = first.reshape(2 * HD, SPAN).T
            att = pl.pallas_call(
                attend_first,
                out_shape=shape(N, SPAN, HD),
                in_specs=[SMEM] + [VMEM] * 3,
                out_specs=VMEM,
                scratch_shapes=[pltpu.VMEM((SPAN, N * PRE), F32)],
                compiler_params=PARAMS,
                name="attend_first",
            )(place, q, held, first)
        else:
            mine, wkv_all = lax.optimization_barrier((mine, wkv_all))
            own_state = pl.pallas_call(
                own_rows,
                out_shape=(shape(ROWS, D), shape(ROWS, HD)) + (shape(ROWS, HD, dtype=F32),) * 3,
                in_specs=[SMEM] + [VMEM] * 5,
                out_specs=(VMEM,) * 5,
                scratch_shapes=[pltpu.VMEM((ROWS, N * PRE), F32)],
                compiler_params=PARAMS,
                name="own_rows",
            )(place, mine, gain, wq_here, held, first)
            att, kv = pl.pallas_call(
                other_rows,
                out_shape=(shape(N, SPAN, HD), shape(SPAN, 2 * HD)),
                in_specs=[SMEM] + [VMEM] * 11,
                out_specs=(VMEM, VMEM),
                scratch_shapes=[pltpu.VMEM((ROWS, D), BF16), pltpu.VMEM((ROWS, N * PRE), F32)],
                compiler_params=PARAMS,
                name="other_rows",
            )(place, other, gain, wq_here, wkv_all, held, first, *own_state)
            late, kv_first, kv = lax.optimization_barrier((sums[0], kv_first, kv))
            sums[0] = late
            both = []
            for here in (kv_first, kv):
                pair = lax.ppermute(here, "kvp", [(i, (i + RING) % N) for i in range(N)])
                heads = jnp.where(g == 0, jnp.stack([here, pair]), jnp.stack([pair, here]))
                both.append(jnp.transpose(heads.reshape(2, SPAN, 2, HD), (2, 0, 1, 3)))
        att = spread(att)
        if moment:
            new_cache = cache_here
            for u in range(NCH):
                new_cache = updated(new_cache, both[u], u, owner)
            new_cache, att = lax.optimization_barrier((new_cache, att))
        own_sum, other_sum = pl.pallas_call(
            mix,
            out_shape=(shape(ROWS, COLS, dtype=F32), shape(ROWS, COLS, dtype=F32)),
            in_specs=[SMEM] + [VMEM] * 3,
            out_specs=(VMEM, VMEM),
            compiler_params=PARAMS,
            name="mix",
        )(place, att, wo_here, x)
        sums.append((own_sum, other_sum))
    outputs = [(mine + swap(other)).astype(BF16) for mine, other in sums]
    return (jnp.stack(outputs)[:, None], new_cache[None])


def solution(mesh):
    in_specs = (
        P("section", "tp", "kvp"),
        P(None, "tp", "kvp"),
        P("section", None),
        P("section", None, "tp", "kvp"),
        P("section", None, "tp", "kvp"),
        P("section", "tp", "kvp"),
        P("section", None, "tp", "kvp", None),
        P("section", "kvp"),
        P(None, "section"),
    )
    out_specs = (P(None, "section", "tp", "kvp"), P("section", None, "tp", "kvp", None))
    return jax.shard_map(body, mesh=mesh, in_specs=in_specs, out_specs=out_specs, check_vma=False)
```

```python
import functools
import math

import jax
import jax.numpy as jnp
from jax import lax
from jax.experimental import pallas as pl
from jax.experimental.pallas import tpu as pltpu
from jax.sharding import PartitionSpec as P

HD = 128
NCH = 2
EPS = 1e-05
N = 16
RING = 8
ROWS = 64
SPAN = 128
PRE = 256
D = 4096
COLS = 256
SCALE = 1.0 / math.sqrt(HD)
LOW = -1e30
MARK = 1024.0
F32 = jnp.float32
BF16 = jnp.bfloat16
RINGS = [list(range(RING)), list(range(RING, N))]
VMEM = pl.BlockSpec(memory_space=pltpu.VMEM)
SMEM = pl.BlockSpec(memory_space=pltpu.SMEM)
PARAMS = pltpu.CompilerParams(vmem_limit_bytes=40 * 1024 * 1024)


def dot(a, b):
    return jnp.dot(a, b, preferred_element_type=F32)


def dot_t(a, b):
    return lax.dot_general(a, b, (((1,), (1,)), ((), ())), preferred_element_type=F32)


def normalise(ref, gain, normed, rows):
    total = jnp.zeros((ROWS, COLS), F32)
    for j in range(N):
        part = ref[j].astype(F32)
        total = total + part * part
    inverse = lax.rsqrt(jnp.sum(total, axis=1, keepdims=True) / D + EPS)
    for j in range(N):
        cols = slice(j * COLS, (j + 1) * COLS)
        normed[rows, cols] = (ref[j].astype(F32) * inverse * gain[:, cols]).astype(BF16)


def half_rows(half):
    return pl.ds(pl.multiple_of(half * ROWS, ROWS), ROWS)


def project_first(place, mine, other, gain, wq, wkv, q_out, kv_out, normed):
    t = place[0]
    normalise(mine, gain, normed, half_rows(t))
    normalise(other, gain, normed, half_rows(1 - t))
    q_out[...] = dot(normed[...], wq[...]).astype(BF16)
    kv = dot_t(wkv[...], normed[...]).astype(BF16)
    for j in range(RING):
        kv_out[j] = kv


def over_prefixes(q, held, scores):
    count = q.shape[0]
    slot = lax.broadcasted_iota(jnp.int32, (1, PRE), 1).astype(F32)
    top = jnp.full((count, PRE), LOW, F32)
    for k in range(RING):
        for o in range(2):
            mark = held[k, o, 0, PRE - 16 : PRE][15:16].astype(F32)
            filled = jnp.where(mark > MARK / 2, mark / MARK, float(PRE))
            filled = jnp.concatenate([filled, filled], axis=1)
            s = dot_t(q, held[k, o, 0]) * SCALE
            s = jnp.where(slot < filled, s, LOW)
            b = (k * 2 + o) * PRE
            scores[:, b : b + PRE] = s
            top = jnp.maximum(top, s)
    top = jnp.max(top, axis=1, keepdims=True)
    total = jnp.zeros((count, PRE), F32)
    acc = jnp.zeros((count, HD), F32)
    for k in range(RING):
        for o in range(2):
            b = (k * 2 + o) * PRE
            e = jnp.exp(scores[:, b : b + PRE] - top)
            total = total + e
            acc = acc + dot(e.astype(BF16), held[k, o, 1])
    return top, jnp.sum(total, axis=1, keepdims=True), acc


def with_spans(start, top, total, acc, spans):
    count = acc.shape[0]
    row = lax.broadcasted_iota(jnp.int32, (count, SPAN), 0) + start
    col = lax.broadcasted_iota(jnp.int32, (count, SPAN), 1)
    spans = list(spans)
    spans[-1] = (jnp.where(col <= row, spans[-1][0], LOW), spans[-1][1])
    peak = top
    for s, _ in spans:
        peak = jnp.maximum(peak, jnp.max(s, axis=1, keepdims=True))
    weight = jnp.exp(top - peak)
    total = total * weight
    acc = acc * weight
    for s, product in spans:
        e = jnp.exp(s - peak)
        total = total + jnp.sum(e, axis=1, keepdims=True)
        acc = acc + product(e.astype(BF16))
    return (acc / total).astype(BF16)


def first_span(q, first):
    keys = jnp.concatenate([first[i] for i in range(4)], axis=0)
    values = jnp.concatenate([first[4 + i] for i in range(4)], axis=0)
    return dot(q, keys) * SCALE, lambda e: dot_t(e, values)


def attend_first(place, q_ref, held, first, wo, out, scores):
    g = place[1]
    q = q_ref[...]
    top, total, acc = over_prefixes(q, held, scores)
    result = with_spans(0, top, total, acc, [first_span(q, first)])
    for j in range(N):
        out[j] = result


def own_rows(place, x, gain, wq, held, first, normed, q_out, top_out, sum_out, acc_out, scores):
    normalise(x, gain, normed, slice(0, ROWS))
    q = dot(normed[...], wq[...]).astype(BF16)
    q_out[...] = q
    top, total, acc = over_prefixes(q, held, scores)
    top_out[...] = jnp.broadcast_to(top, (ROWS, HD))
    sum_out[...] = jnp.broadcast_to(total, (ROWS, HD))
    acc_out[...] = acc


def other_rows(
    place, x, gain, wq, wkv, held, first, normed_own, q_own, top_own, sum_own, acc_own, out, kv, normed, scores
):
    t, g = place[0], place[1]
    normalise(x, gain, normed, slice(0, ROWS))
    q = dot(normed[...], wq[...]).astype(BF16)
    both = jnp.concatenate([normed_own[...], normed[...]], axis=0)
    both = dot_t(both, wkv[...]).astype(BF16)
    kv[half_rows(t), :] = both[0:ROWS]
    kv[half_rows(1 - t), :] = both[ROWS:SPAN]
    top, total, acc = over_prefixes(q, held, scores)
    keys, values = kv[:, 0:HD], kv[:, HD : 2 * HD]
    parts = (
        (t, q_own[...], top_own[:, 0:1], sum_own[:, 0:1], acc_own[...]),
        (1 - t, q, top, total, acc),
    )
    for half, q, top, total, acc in parts:
        spans = [first_span(q, first), (dot_t(q, keys) * SCALE, lambda e: dot(e, values))]
        result = with_spans(half * ROWS, top, total, acc, spans)
        for j in range(N):
            out[j, half_rows(half), :] = result


def mix(place, att, wo, x_ref, mine, other):
    t = place[0]
    acc = jnp.zeros((SPAN, COLS), F32)
    for j in range(N):
        acc = acc + dot(att[j], wo[j * HD : (j + 1) * HD, :])
    top, bottom = acc[0:ROWS], acc[ROWS:SPAN]
    mine[...] = x_ref[...].astype(F32) + jnp.where(t == 0, top, bottom)
    other[...] = jnp.where(t == 0, bottom, top)


def spread(block):
    return lax.all_to_all(block, "kvp", 0, 0, tiled=True)


def swap(block):
    return lax.ppermute(block, "tp", [(0, 1), (1, 0)])


def onward(block, cross):
    route = [(i, (i ^ cross) + 2) for i in range(30)]
    return lax.ppermute(block, ("section", "tp"), route)


def shape(*dims, dtype=BF16):
    return jax.ShapeDtypeStruct(dims, dtype)


def body(entering, feed, gain, wq, wkv, wo, cache, prefix_len, owner):
    shard_id = lax.axis_index("kvp")
    section_id = lax.axis_index("section")
    g = shard_id // RING
    place = jnp.stack([lax.axis_index("tp"), g]).astype(jnp.int32)
    filled = prefix_len[0, 0]
    wq_here, wkv_here, wo_here = wq[0, :, 0, :], wkv[0, :, 0, :], wo[0]
    cache_here = cache[0]

    prefix = cache_here[:, :, :PRE, :]
    last = prefix[0:1, :, PRE - 1 : PRE]
    last = jnp.where(filled < PRE, (filled.astype(F32) * MARK).astype(BF16), last)
    prefix = lax.dynamic_update_slice(prefix, last, (0, 0, PRE - 1, 0))
    own = lax.dynamic_index_in_dim(prefix, g, 1, False)
    give = lax.dynamic_index_in_dim(prefix, 1 - g, 1, False)
    got = lax.ppermute(give, "kvp", [(i, (i + RING) % N) for i in range(N)])
    held = lax.all_gather(jnp.stack([own, got]), "kvp", axis_index_groups=RINGS)

    wkv_t = wkv_here.T

    def updated(cache_now, fresh, moment, owner):
        start = filled
        for u in range(moment):
            start = start + jnp.where(owner[u, 0] == shard_id, SPAN, 0).astype(jnp.int32)
        changed = lax.dynamic_update_slice(cache_now, fresh, (0, 0, start, 0))
        return jnp.where(owner[moment, 0] == shard_id, changed, cache_now)

    sums = []
    x = entering[0]
    for moment in range(NCH):
        if moment:
            passed = (onward(own_sum, 0) + onward(other_sum, 1)).astype(BF16)
            x = jnp.where(section_id == 0, feed[moment - 1], passed)
        mine = spread(jnp.broadcast_to(x[None], (N, ROWS, COLS)))
        other = swap(mine)
        if moment == 0:
            q, kv = pl.pallas_call(
                project_first,
                out_shape=(shape(SPAN, HD), shape(RING, 32, SPAN)),
                in_specs=[SMEM] + [VMEM] * 5,
                out_specs=(VMEM, VMEM),
                scratch_shapes=[pltpu.VMEM((SPAN, D), BF16)],
                compiler_params=PARAMS,
                name="project_first",
            )(place, mine, other, gain, wq_here, wkv_t)
            first = lax.all_to_all(kv, "kvp", 0, 0, tiled=True, axis_index_groups=RINGS)
            wkv_late, first = lax.optimization_barrier((wkv_t, first))
            wkv_all = lax.all_gather(wkv_late, "kvp", axis_index_groups=RINGS)
            wkv_all = wkv_all.reshape(2 * HD, D)
            kv_first = first.reshape(2 * HD, SPAN).T
            att = pl.pallas_call(
                attend_first,
                out_shape=shape(N, SPAN, HD),
                in_specs=[SMEM] + [VMEM] * 4,
                out_specs=VMEM,
                scratch_shapes=[pltpu.VMEM((SPAN, N * PRE), F32)],
                compiler_params=PARAMS,
                name="attend_first",
            )(place, q, held, first, wo_here)
        else:
            mine, wkv_all = lax.optimization_barrier((mine, wkv_all))
            own_state = pl.pallas_call(
                own_rows,
                out_shape=(shape(ROWS, D), shape(ROWS, HD)) + (shape(ROWS, HD, dtype=F32),) * 3,
                in_specs=[SMEM] + [VMEM] * 5,
                out_specs=(VMEM,) * 5,
                scratch_shapes=[pltpu.VMEM((ROWS, N * PRE), F32)],
                compiler_params=PARAMS,
                name="own_rows",
            )(place, mine, gain, wq_here, held, first)
            att, kv = pl.pallas_call(
                other_rows,
                out_shape=(shape(N, SPAN, HD), shape(SPAN, 2 * HD)),
                in_specs=[SMEM] + [VMEM] * 11,
                out_specs=(VMEM, VMEM),
                scratch_shapes=[pltpu.VMEM((ROWS, D), BF16), pltpu.VMEM((ROWS, N * PRE), F32)],
                compiler_params=PARAMS,
                name="other_rows",
            )(place, other, gain, wq_here, wkv_all, held, first, *own_state)
            late, kv_first, kv = lax.optimization_barrier((sums[0], kv_first, kv))
            sums[0] = late
            both = []
            for here in (kv_first, kv):
                pair = lax.ppermute(here, "kvp", [(i, (i + RING) % N) for i in range(N)])
                heads = jnp.where(g == 0, jnp.stack([here, pair]), jnp.stack([pair, here]))
                both.append(jnp.transpose(heads.reshape(2, SPAN, 2, HD), (2, 0, 1, 3)))
        att = spread(att)
        if moment:
            new_cache = cache_here
            for u in range(NCH):
                new_cache = updated(new_cache, both[u], u, owner)
            new_cache, att = lax.optimization_barrier((new_cache, att))
        own_sum, other_sum = pl.pallas_call(
            mix,
            out_shape=(shape(ROWS, COLS, dtype=F32), shape(ROWS, COLS, dtype=F32)),
            in_specs=[SMEM] + [VMEM] * 3,
            out_specs=(VMEM, VMEM),
            compiler_params=PARAMS,
            name="mix",
        )(place, att, wo_here, x)
        sums.append((own_sum, other_sum))
    outputs = [(mine + swap(other)).astype(BF16) for mine, other in sums]
    return (jnp.stack(outputs)[:, None], new_cache[None])


def solution(mesh):
    in_specs = (
        P("section", "tp", "kvp"),
        P(None, "tp", "kvp"),
        P("section", None),
        P("section", None, "tp", "kvp"),
        P("section", None, "tp", "kvp"),
        P("section", "tp", "kvp"),
        P("section", None, "tp", "kvp", None),
        P("section", "kvp"),
        P(None, "section"),
    )
    out_specs = (P(None, "section", "tp", "kvp"), P("section", None, "tp", "kvp", None))
    return jax.shard_map(body, mesh=mesh, in_specs=in_specs, out_specs=out_specs, check_vma=False)
```
